32 devices in a mesh: grp: 2 (over y), sp: 4 (over z), ch: 2 (over x), sub: 2 (over core).
Axes of the slice: x: 2, y: 2, z: 4, core: 2. Of those that a mesh axis runs over, the one named last changes fastest.
Arguments:
- volume: bfloat16 [64, 32, 64, 128], P('ch', ('grp', 'sp'), 'sub'), parts along dimension 1, may hold values from -6 to 6
- kernel: bfloat16 [128, 64, 64], P(None, 'ch'), may hold values from -0.09375 to 0.09375
- cotangent: bfloat16 [128, 16, 2048], P('ch', ('grp', 'sp'), 'sub'), parts along dimension 1, may hold values from -6 to 6
Outputs:
- features: bfloat16 [128, 16, 2048], P('ch', ('grp', 'sp'), 'sub'), parts along dimension 1
- volume_grad: bfloat16 [64, 32, 64, 128], P('ch', ('grp', 'sp'), 'sub'), parts along dimension 1
- kernel_grad: float32 [256, 64, 64], P(('grp', 'sp', 'sub'), 'ch'), parts along dimension 0
The draws below stay inside these ranges and needn't reach their ends.
There are 2 independent parts, one for each index of `grp`. The reference program is written for one: setup_inputs(seed, part) draws one part's arguments, and reference() takes and returns one part's arrays. A program takes and returns all parts, laid end to end along the dimension named above; an argument that names none is the same for every part. Nothing has to cross between parts.
All inputs are finite; a program needn't handle non-finite values.
Results may differ from the reference program's by a relative error of at most 0.0034.
Values may be sent and summed in bfloat16 or wider, within the bound.
A program may use at most 128 MiB of HBM per device.

```python
import jax
import jax.numpy as jnp
from jax import lax

CIN = 64
COUT = 128
WID = 128
DEPTH = 16
HEIGHT = 64


def raised(values, stream_key, source, target, shards_of, factor):
    def block_of(axis_at):
        return (jnp.arange(values.shape[axis_at]) // (values.shape[axis_at] // shards_of)).reshape((-1,) + (1,) * (values.ndim - 1 - axis_at))

    near = jax.random.permutation(stream_key, shards_of)[block_of(target)]
    far = (block_of(target) + shards_of // 2) % shards_of
    return jnp.where((block_of(source) == near) | (block_of(source) == far), factor * values, values)


def steps_of(stream_key, extent, pieces, least, largest):
    loudness, own = 1.0, jax.random.fold_in(stream_key, 6)
    for position, shards_of in pieces:
        steps = jnp.exp(jax.random.uniform(jax.random.fold_in(own, position), (shards_of,), jnp.float32, least / len(pieces), largest / len(pieces)))
        loudness = loudness * jnp.repeat(steps, extent[position] // shards_of).reshape([-1 if axis == position else 1 for axis in range(len(extent))])
    return loudness


def centred(key, dims, spread, most, cuts=(), held_as=jnp.bfloat16):
    loudness = steps_of(key, dims, cuts, -0.22, 0.18) if cuts else 1.0
    values = jax.random.normal(key, dims, jnp.float32) * spread * loudness
    return jnp.minimum(jnp.maximum(values, -most), most).astype(held_as)


def bell_draw_with(key, dims, spread, most, pieces, heavy, kind=jnp.bfloat16):
    values = spread * jax.random.normal(key, dims, jnp.float32)
    if pieces:
        values = values * steps_of(key, dims, pieces, -0.22, 0.18)
    return jnp.clip(raised(values, jax.random.fold_in(key, 3), *heavy), -most, most).astype(kind)


def setup_inputs(seed: int = 0, part: int = 0) -> dict:
    key_list = jax.random.split(jax.random.key(seed), 4)
    part_keys = jax.random.split(jax.random.fold_in(key_list[3], part), 4)
    return {
        "volume": centred(part_keys[0], (CIN, DEPTH, HEIGHT, WID), 1.0, 6.0, ((0, 2), (1, 4), (2, 2))),
        "kernel": centred(key_list[1], (COUT, CIN, 64), (CIN * 64) ** -0.5, 0.09375, ((1, 2),)),
        "cotangent": bell_draw_with(part_keys[2], (COUT, DEPTH // 2, (HEIGHT // 2) * (WID // 2)), 1.0, 6.0, ((0, 2), (1, 4), (2, 2)), (1, 0, 4, 2.0)),
    }


def strided_conv(inputs, filters):
    result = lax.conv_general_dilated(inputs[None], filters, (2, 2, 2), ((1, 1), (1, 1), (1, 1)), dimension_numbers=('NCDHW', 'OIDHW', 'NCDHW'), precision=lax.Precision.HIGHEST)
    return result[0]

def reference(volume, kernel, cotangent):
    n_out = kernel.shape[0]
    n_in = kernel.shape[1]
    inputs = volume.astype(jnp.float32)
    filters = kernel.reshape(n_out, n_in, 4, 4, 4).astype(jnp.float32)
    outputs, pullback = jax.vjp(strided_conv, inputs, filters)
    out_shape = outputs.shape
    grad_out = cotangent.astype(jnp.float32).reshape(out_shape)
    grad_in, grad_filters = pullback(grad_out)
    features = outputs.reshape(out_shape[0], out_shape[1], out_shape[2] * out_shape[3]).astype(jnp.bfloat16)
    return (features, grad_in.astype(jnp.bfloat16), grad_filters.reshape(n_out, n_in, 64))
```

```python
import functools

import jax
import jax.numpy as jnp
from jax import lax
from jax.experimental import pallas as pl
from jax.experimental.pallas import tpu as pltpu
from jax.sharding import PartitionSpec as P

MESH = pl.DeviceIdType.MESH
F32 = jnp.float32
BF16 = jnp.bfloat16


def kernel_body(
    nz, nx, vol, wts, cot, feat, vgrad, kgrad,
    halo, split, edge_out, edge_in, cols, gbuf, fsum, fsend, frecv, kpart, krecv, ksend, kzin, wide, rows32, wt_t,
    v_send, v_recv, g_send, g_recv, gz_send, gz_recv, e_send, e_recv, ge_sem, f_send, f_recv, ks_sem, kz_send, kz_recv, own_sem,
):
    z = lax.axis_index("sp")
    x = lax.axis_index("ch")
    s = lax.axis_index("sub")
    other = 1 - s
    cin = vol.shape[0]
    high = vol.shape[2]
    n_out = wts.shape[0]
    local_out = cot.shape[1]
    area = cot.shape[2]
    tiles = area // 128
    taps = 16 * cin
    has_low = z > 0
    has_high = z < nz - 1

    for side in (0, 128 + area):
        gbuf[:, :, side : side + 128] = jnp.zeros((4, n_out, 128), BF16)

    @pl.when(jnp.logical_not(has_low))
    def _():
        halo[0] = jnp.zeros(halo.shape[1:], BF16)
        gbuf[0] = jnp.zeros(gbuf.shape[1:], BF16)

    @pl.when(jnp.logical_not(has_high))
    def _():
        halo[1] = jnp.zeros(halo.shape[1:], BF16)
        gbuf[3] = jnp.zeros(gbuf.shape[1:], BF16)

    barrier = pltpu.get_barrier_semaphore()
    for k in range(1, nz):
        pl.semaphore_signal(barrier, 1, device_id={"sp": lax.rem(z + k, nz)}, device_id_type=MESH)
    for k in range(1, nx):
        pl.semaphore_signal(barrier, 1, device_id={"ch": lax.rem(x + k, nx)}, device_id_type=MESH)
    pl.semaphore_signal(barrier, 1, device_id={"sub": other}, device_id_type=MESH)
    pl.semaphore_wait(barrier, nz + nx - 1)

    def remote(src, dst, send, recv, target):
        return pltpu.make_async_remote_copy(
            src_ref=src, dst_ref=dst, send_sem=send, recv_sem=recv, device_id=target, device_id_type=MESH
        )

    low = jnp.maximum(z - 1, 0)
    up = jnp.minimum(z + 1, nz - 1)
    v_down = remote(vol.at[:, 0], halo.at[1], v_send.at[0], v_recv.at[1], {"sp": low})
    v_up = remote(vol.at[:, 3], halo.at[0], v_send.at[1], v_recv.at[0], {"sp": up})
    pl.when(has_low)(v_down.start)
    pl.when(has_high)(v_up.start)

    def g_rows(owner):
        return gbuf.at[pl.ds(1, 2), pl.ds(pl.multiple_of(owner * local_out, local_out), local_out), pl.ds(128, area)]

    g_copies = []
    for k in range(1, nx):
        g_copies.append(remote(cot, g_rows(x), g_send.at[k - 1], g_recv.at[k - 1], {"ch": lax.rem(x + k, nx)}))
        g_copies[-1].start()
    own = pltpu.make_async_copy(cot, g_rows(x), own_sem)
    own.start()

    k_at = lax.broadcasted_iota(jnp.int32, (128, 128), 0)
    l_at = lax.broadcasted_iota(jnp.int32, (128, 128), 1)
    pick = [
        (k_at == 2 * (l_at % 64) + (l_at // 64 + 2 * half) - 1).astype(BF16) for half in range(2)
    ]
    first = lax.broadcasted_iota(jnp.int32, (cin, 128), 1) < 64

    def splits(plane, cells):
        flat = cells.reshape(cin * high, 128)
        for half in range(2):
            split[plane, half] = jnp.dot(flat, pick[half], preferred_element_type=F32)
            rim = jnp.where(
                s == 0,
                split.at[plane, half][pl.ds(high - 1, cin, stride=high), :],
                split.at[plane, half][pl.ds(0, cin, stride=high), :],
            )
            edge_out[plane, half] = rim.astype(BF16)

    def own_split(i, _):
        splits(i + 1, vol[:, i])
        return 0

    lax.fori_loop(0, 4, own_split, 0)

    def edge_copy(index, start, count):
        return remote(
            edge_out.at[pl.ds(start, count)], edge_in.at[pl.ds(start, count)],
            e_send.at[index], e_recv.at[index], {"sub": other},
        )

    e_own = edge_copy(0, 1, 4)
    e_own.start()

    own.wait()
    for k in range(1, nx):
        g_copies[k - 1].wait_send()
        origin = lax.rem(x + nx - k, nx)
        remote(cot, g_rows(origin), g_send.at[k - 1], g_recv.at[k - 1], {"ch": origin}).wait_recv()

    def g_plane(at):
        return gbuf.at[at, :, pl.ds(128, area)]

    g_down = remote(g_plane(1), g_plane(3), gz_send.at[0], gz_recv.at[1], {"sp": low})
    g_up = remote(g_plane(2), g_plane(0), gz_send.at[1], gz_recv.at[0], {"sp": up})
    pl.when(has_low)(g_down.start)
    pl.when(has_high)(g_up.start)

    def build(plane):
        for half in range(2):
            rim = edge_in[plane, half].astype(F32)
            above = jnp.where(s == 1, rim, 0.0)
            below = jnp.where(s == 0, rim, 0.0)

            def row(j):
                if j < 0:
                    return above
                if j >= high:
                    return below
                return split.at[plane, half][pl.ds(j, cin, stride=high), :]

            for b in range(4):
                for t in range(tiles):
                    a_row, b_row = row(4 * t + b - 1), row(4 * t + b + 1)
                    left = jnp.where(first, a_row, pltpu.roll(b_row, 64, 1))
                    right = jnp.where(first, pltpu.roll(a_row, 64, 1), b_row)
                    cols[plane, b, 2 * half, :, t * 128 : t * 128 + 128] = left.astype(BF16)
                    cols[plane, b, 2 * half + 1, :, t * 128 : t * 128 + 128] = right.astype(BF16)

    def build_own(i, _):
        build(i + 1)
        return 0

    e_own.wait()
    lax.fori_loop(0, 4, build_own, 0)

    @pl.when(has_low)
    def _():
        v_down.wait_send()
        v_up.wait_recv()

    @pl.when(has_high)
    def _():
        v_up.wait_send()
        v_down.wait_recv()

    def halo_split(i, _):
        splits(5 * i, halo[i])
        return 0

    lax.fori_loop(0, 2, halo_split, 0)
    e_low, e_high = edge_copy(1, 0, 1), edge_copy(2, 5, 1)
    e_low.start()
    e_high.start()

    for odd in range(2):
        for place in range(2):
            a = (3, 1, 2, 0)[2 * odd + place]
            block = wts[:, a * taps : (a + 1) * taps].astype(F32)
            wt_t[odd, :, place * n_out : (place + 1) * n_out] = block.T.astype(BF16)

    e_low.wait()
    e_high.wait()

    def build_halo(i, _):
        build(5 * i)
        return 0

    lax.fori_loop(0, 2, build_halo, 0)

    def forward(step, _):
        d, at = step // (area // 256), step % (area // 256)
        lanes = pl.ds(pl.multiple_of(at * 256, 256), 256)
        block = cols[pl.ds(2 * d, 4), :, :, :, lanes].reshape(4 * taps, 256)
        part = jnp.dot(wts[...], block, preferred_element_type=F32)
        fsum[d, :, lanes] = part
        fsend[d, :, lanes] = part.astype(BF16)
        return 0

    lax.fori_loop(0, 2 * (area // 256), forward, 0)

    def out_rows(ref, owner):
        return ref.at[:, pl.ds(pl.multiple_of(owner * local_out, local_out), local_out), :]

    f_copies = []
    for k in range(1, nx):
        peer = lax.rem(x + k, nx)
        f_copies.append(remote(out_rows(fsend, peer), frecv.at[k - 1], f_send.at[k - 1], f_recv.at[k - 1], {"ch": peer}))
        f_copies[-1].start()

    rows = n_out // (2 * nz)

    def kernel_part(a, _):
        total = 0.0
        for d in range(2):
            total += lax.dot_general(
                gbuf[1 + d, :, 128 : 128 + area],
                cols[2 * d + a].reshape(taps, area),
                (((1,), (1,)), ((), ())),
                preferred_element_type=F32,
            )
        for block in range(2 * nz):
            kpart[block // 2, block % 2, :, pl.ds(pl.multiple_of(a * taps, 128), taps)] = total[block * rows : (block + 1) * rows]
        return 0

    lax.fori_loop(0, 4, kernel_part, 0)
    k_pair = remote(kpart.at[:, other], krecv, ks_sem.at[0], ks_sem.at[1], {"sub": other})
    k_pair.start()

    @pl.when(has_low)
    def _():
        g_down.wait_send()
        g_up.wait_recv()

    @pl.when(has_high)
    def _():
        g_up.wait_send()
        g_down.wait_recv()

    g_edge = remote(
        gbuf.at[:, :, pl.ds(pl.multiple_of(jnp.where(s == 0, area, 128), 128), 128)],
        gbuf.at[:, :, pl.ds(pl.multiple_of(jnp.where(s == 0, 0, 128 + area), 128), 128)],
        ge_sem.at[0], ge_sem.at[1], {"sub": other},
    )
    g_edge.start()

    k_pair.wait_send()
    remote(kpart.at[:, other], krecv, ks_sem.at[0], ks_sem.at[1], {"sub": other}).wait_recv()
    for block in range(nz):
        mine = jnp.where(s == 0, kpart[block, 0], kpart[block, 1]) + krecv[block]
        krecv[block] = mine
        ksend[block, 0:rows, :] = mine.astype(BF16)
    k_copies = []
    for k in range(1, nz):
        peer = lax.rem(z + k, nz)
        k_copies.append(remote(ksend.at[peer], kzin.at[k - 1], kz_send.at[k - 1], kz_recv.at[k - 1], {"sp": peer}))
        k_copies[-1].start()

    g_edge.wait_send()
    remote(
        gbuf.at[:, :, pl.ds(0, 128)],
        gbuf.at[:, :, pl.ds(pl.multiple_of(jnp.where(s == 0, 128 + area, 0), 128), 128)],
        ge_sem.at[0], ge_sem.at[1], {"sub": other},
    ).wait_recv()

    lane = lax.broadcasted_iota(jnp.int32, (cin, 128), 1) % 64
    inner_low, inner_high = lane > 0, lane < 63
    weave = (l_at == 2 * (k_at % 64) + k_at // 64).astype(BF16)

    def volume_plane(i, _):
        block = gbuf[pl.ds((i + 1) // 2, 2)].reshape(2 * n_out, 256 + area)
        wide[...] = jnp.dot(wt_t[i % 2], block, preferred_element_type=F32)

        def term(b, r, t):
            lanes = slice(t * 128, t * 128 + 128)

            def tap(e):
                return wide[(4 * b + e) * cin : (4 * b + e + 1) * cin, lanes]

            if r == 0:
                return tap(1) + jnp.where(inner_low, pltpu.roll(tap(3), 1, 1), 0.0)
            return tap(2) + jnp.where(inner_high, pltpu.roll(tap(0), 127, 1), 0.0)

        for q in range(2):
            kept = [None, None]
            for t in range(1, tiles + 1):
                both = []
                for r in range(2):
                    if q == 0:
                        before = pltpu.roll(term(3, r, t - 1), 64, 1) if kept[r] is None else kept[r]
                        after = pltpu.roll(term(3, r, t), 64, 1)
                        base = term(1, r, t)
                    else:
                        before = pltpu.roll(term(0, r, t), 64, 1) if kept[r] is None else kept[r]
                        after = pltpu.roll(term(0, r, t + 1), 64, 1)
                        base = term(2, r, t)
                    kept[r] = after
                    both.append(base + jnp.where(first, before, after))
                n = 2 * (t - 1)
                rows32[pl.ds(2 * n + q, cin, stride=high), :] = jnp.where(first, both[0], pltpu.roll(both[1], 64, 1))
                rows32[pl.ds(2 * n + 2 + q, cin, stride=high), :] = jnp.where(first, pltpu.roll(both[0], 64, 1), both[1])
        woven = jnp.dot(rows32[...].astype(BF16), weave, preferred_element_type=F32)
        vgrad[:, i] = woven.astype(BF16).reshape(cin, high, 128)
        return 0

    lax.fori_loop(0, 4, volume_plane, 0)

    for d in range(2):
        total = fsum[d, pl.ds(pl.multiple_of(x * local_out, local_out), local_out), :]
        for k in range(1, nx):
            if d == 0:
                f_copies[k - 1].wait()
            total = total + frecv[k - 1, d].astype(F32)
        feat[d] = total.astype(BF16)

    result = krecv[z]
    for k in range(1, nz):
        k_copies[k - 1].wait()
        result = result + kzin[k - 1, 0:rows, :].astype(F32)
    kgrad[...] = result


def body(volume, kernel, cotangent):
    n_out, cin = kernel.shape[:2]
    nz, nx = lax.axis_size("sp"), lax.axis_size("ch")
    local_out, depth, area = cotangent.shape
    high = volume.shape[2]
    rows = n_out // (2 * nz)
    padded_rows = -(-rows // 16) * 16
    weights = kernel.transpose(0, 2, 1).reshape(n_out, 64 * cin)
    grads = cotangent.transpose(1, 0, 2)
    vmem = pl.BlockSpec(memory_space=pltpu.VMEM)
    dma = pltpu.SemaphoreType.DMA
    feat, vgrad, kgrad = pl.pallas_call(
        functools.partial(kernel_body, nz, nx),
        out_shape=(
            jax.ShapeDtypeStruct((depth, local_out, area), BF16),
            jax.ShapeDtypeStruct(volume.shape, BF16),
            jax.ShapeDtypeStruct((rows, 64 * cin), F32),
        ),
        in_specs=[vmem] * 3,
        out_specs=[vmem] * 3,
        scratch_shapes=[
            pltpu.VMEM((2, cin, high, 128), BF16),
            pltpu.VMEM((6, 2, cin * high, 128), F32),
            pltpu.VMEM((6, 2, cin, 128), BF16),
            pltpu.VMEM((6, 2, cin, 128), BF16),
            pltpu.VMEM((6, 4, 4, cin, area), BF16),
            pltpu.VMEM((4, n_out, 256 + area), BF16),
            pltpu.VMEM((depth, n_out, area), F32),
            pltpu.VMEM((depth, n_out, area), BF16),
            pltpu.VMEM((nx - 1, depth, local_out, area), BF16),
            pltpu.VMEM((nz, 2, rows, 64 * cin), F32),
            pltpu.VMEM((nz, rows, 64 * cin), F32),
            pltpu.VMEM((nz, padded_rows, 64 * cin), BF16),
            pltpu.VMEM((nz - 1, padded_rows, 64 * cin), BF16),
            pltpu.VMEM((16 * cin, 256 + area), F32),
            pltpu.VMEM((cin * high, 128), F32),
            pltpu.VMEM((2, 16 * cin, 2 * n_out), BF16),
            dma((2,)), dma((2,)),
            dma((nx - 1,)), dma((nx - 1,)),
            dma((2,)), dma((2,)),
            dma((3,)), dma((3,)),
            dma((2,)),
            dma((nx - 1,)), dma((nx - 1,)),
            dma((2,)),
            dma((nz - 1,)), dma((nz - 1,)),
            dma,
        ],
        compiler_params=pltpu.CompilerParams(
            collective_id=0, has_side_effects=True, vmem_limit_bytes=56 * 1024 * 1024
        ),
    )(volume, weights, grads)
    features = feat.transpose(1, 0, 2)
    kernel_grad = kgrad.reshape(rows, 64, cin).transpose(0, 2, 1)
    return (features, vgrad, kernel_grad)


def solution(mesh):
    return jax.shard_map(
        body,
        mesh=mesh,
        in_specs=(
            P("ch", ("grp", "sp"), "sub", None),
            P(None, "ch", None),
            P("ch", ("grp", "sp"), "sub"),
        ),
        out_specs=(
            P("ch", ("grp", "sp"), "sub"),
            P("ch", ("grp", "sp"), "sub", None),
            P(("grp", "sp", "sub"), "ch", None),
        ),
        check_vma=False,
    )
```

```python
import functools

import jax
import jax.numpy as jnp
from jax import lax
from jax.experimental import pallas as pl
from jax.experimental.pallas import tpu as pltpu
from jax.sharding import PartitionSpec as P

MESH = pl.DeviceIdType.MESH
F32 = jnp.float32
BF16 = jnp.bfloat16


def kernel_body(
    nz, nx, vol, wts, cot, feat, vgrad, kgrad,
    halo, split, edge_out, edge_in, cols, gbuf, fsum, fsend, frecv, kpart, krecv, ksend, kzin, wide, rows32, wt_t,
    v_send, v_recv, g_send, g_recv, gz_send, gz_recv, e_send, e_recv, ge_sem, f_send, f_recv, ks_sem, kz_send, kz_recv, own_sem,
):
    z = lax.axis_index("sp")
    x = lax.axis_index("ch")
    s = lax.axis_index("sub")
    other = 1 - s
    cin = vol.shape[0]
    high = vol.shape[2]
    n_out = wts.shape[0]
    local_out = cot.shape[1]
    area = cot.shape[2]
    tiles = area // 128
    taps = 16 * cin
    pitch = high + 8
    has_low = z > 0
    has_high = z < nz - 1

    for side in (0, 128 + area):
        gbuf[:, :, side : side + 128] = jnp.zeros((4, n_out, 128), BF16)

    @pl.when(jnp.logical_not(has_low))
    def _():
        halo[0] = jnp.zeros(halo.shape[1:], BF16)
        gbuf[0] = jnp.zeros(gbuf.shape[1:], BF16)

    @pl.when(jnp.logical_not(has_high))
    def _():
        halo[1] = jnp.zeros(halo.shape[1:], BF16)
        gbuf[3] = jnp.zeros(gbuf.shape[1:], BF16)

    barrier = pltpu.get_barrier_semaphore()
    for k in range(1, nz):
        pl.semaphore_signal(barrier, 1, device_id={"sp": lax.rem(z + k, nz)}, device_id_type=MESH)
    for k in range(1, nx):
        pl.semaphore_signal(barrier, 1, device_id={"ch": lax.rem(x + k, nx)}, device_id_type=MESH)
    pl.semaphore_signal(barrier, 1, device_id={"sub": other}, device_id_type=MESH)

    k_at = lax.broadcasted_iota(jnp.int32, (128, 128), 0)
    l_at = lax.broadcasted_iota(jnp.int32, (128, 128), 1)
    pick = [
        (k_at == 2 * (l_at % 64) + (l_at // 64 + 2 * half) - 1).astype(BF16) for half in range(2)
    ]
    first = lax.broadcasted_iota(jnp.int32, (cin, 128), 1) < 64

    def splits(plane, cells):
        flat = cells.reshape(cin * high, 128)
        for half in range(2):
            value = jnp.dot(flat, pick[half], preferred_element_type=F32)
            for c in range(cin):
                split[plane, half, c * pitch : c * pitch + high, :] = value[c * high : (c + 1) * high]
            rim = jnp.where(
                s == 0,
                split.at[plane, half][pl.ds(high - 1, cin, stride=pitch), :],
                split.at[plane, half][pl.ds(0, cin, stride=pitch), :],
            )
            edge_out[plane, half] = rim.astype(BF16)

    def own_split(i, _):
        splits(i + 1, vol[:, i])
        return 0

    lax.fori_loop(0, 4, own_split, 0)

    pl.semaphore_wait(barrier, nz + nx - 1)

    def remote(src, dst, send, recv, target):
        return pltpu.make_async_remote_copy(
            src_ref=src, dst_ref=dst, send_sem=send, recv_sem=recv, device_id=target, device_id_type=MESH
        )

    low = jnp.maximum(z - 1, 0)
    up = jnp.minimum(z + 1, nz - 1)
    v_down = remote(vol.at[:, 0], halo.at[1], v_send.at[0], v_recv.at[1], {"sp": low})
    v_up = remote(vol.at[:, 3], halo.at[0], v_send.at[1], v_recv.at[0], {"sp": up})
    pl.when(has_low)(v_down.start)
    pl.when(has_high)(v_up.start)

    def g_rows(owner):
        return gbuf.at[pl.ds(1, 2), pl.ds(pl.multiple_of(owner * local_out, local_out), local_out), pl.ds(128, area)]

    g_copies = []
    for k in range(1, nx):
        g_copies.append(remote(cot, g_rows(x), g_send.at[k - 1], g_recv.at[k - 1], {"ch": lax.rem(x + k, nx)}))
        g_copies[-1].start()
    own = pltpu.make_async_copy(cot, g_rows(x), own_sem)
    own.start()

    def edge_copy(index, start, count):
        return remote(
            edge_out.at[pl.ds(start, count)], edge_in.at[pl.ds(start, count)],
            e_send.at[index], e_recv.at[index], {"sub": other},
        )

    e_own = edge_copy(0, 1, 4)
    e_own.start()

    def build(plane):
        for half in range(2):
            rim = edge_in[plane, half].astype(F32)
            above = jnp.where(s == 1, rim, 0.0)
            below = jnp.where(s == 0, rim, 0.0)

            def row(j):
                if j < 0:
                    return above
                if j >= high:
                    return below
                return split.at[plane, half][pl.ds(j, cin, stride=pitch), :]

            for start in (-1, 0):
                a_row = row(start)
                a_turned = pltpu.roll(a_row, 64, 1)
                for j in range(start, high - 1, 2):
                    b_row = row(j + 2)
                    b_turned = pltpu.roll(b_row, 64, 1)
                    b, t = (j + 1) % 4, (j + 1) // 4
                    lanes = slice(t * 128, t * 128 + 128)
                    cols[plane, b, 2 * half, :, lanes] = jnp.where(first, a_row, b_turned).astype(BF16)
                    cols[plane, b, 2 * half + 1, :, lanes] = jnp.where(first, a_turned, b_row).astype(BF16)
                    a_row, a_turned = b_row, b_turned

    def g_plane(at):
        return gbuf.at[at, :, pl.ds(128, area)]

    g_down = remote(g_plane(1), g_plane(3), gz_send.at[0], gz_recv.at[1], {"sp": low})
    g_up = remote(g_plane(2), g_plane(0), gz_send.at[1], gz_recv.at[0], {"sp": up})
    def spread():
        own.wait()
        for k in range(1, nx):
            g_copies[k - 1].wait_send()
            origin = lax.rem(x + nx - k, nx)
            remote(cot, g_rows(origin), g_send.at[k - 1], g_recv.at[k - 1], {"ch": origin}).wait_recv()
        pl.when(has_low)(g_down.start)
        pl.when(has_high)(g_up.start)

    def build_own(i, _):
        pl.when(i == 2)(spread)
        build(i + 1)
        return 0

    e_own.wait()
    lax.fori_loop(0, 4, build_own, 0)

    rows = n_out // (2 * nz)

    def kernel_part(group, index, a):
        total = 0.0
        for d in range(2):
            total += lax.dot_general(
                gbuf[1 + d, :, 128 : 128 + area],
                cols[2 * d + a].reshape(taps, area),
                (((1,), (1,)), ((), ())),
                preferred_element_type=F32,
            )
        lanes = pl.ds(pl.multiple_of(index * taps, 128), taps)
        for block in range(2 * nz):
            kpart[group, block // 2, block % 2, :, lanes] = total[block * rows : (block + 1) * rows]

    def k_pair(group):
        return remote(
            kpart.at[group, :, other], krecv.at[group], ks_sem.at[0, group], ks_sem.at[1, group], {"sub": other}
        )

    def k_copy(group, k):
        peer = lax.rem(z + k, nz)
        return remote(
            ksend.at[group, peer], kzin.at[group, k - 1],
            kz_send.at[group, k - 1], kz_recv.at[group, k - 1], {"sp": peer},
        )

    def k_reduce(group):
        k_pair(group).wait()
        for block in range(nz):
            mine = jnp.where(s == 0, kpart[group, block, 0], kpart[group, block, 1]) + krecv[group, block]
            krecv[group, block] = mine
            ksend[group, block, 0:rows, :] = mine.astype(BF16)
        for k in range(1, nz):
            k_copy(group, k).start()

    def inner_parts(index, _):
        kernel_part(0, index, 1 + index)
        return 0

    lax.fori_loop(0, 2, inner_parts, 0)
    k_pair(0).start()

    @pl.when(has_low)
    def _():
        v_down.wait_send()
        v_up.wait_recv()

    @pl.when(has_high)
    def _():
        v_up.wait_send()
        v_down.wait_recv()

    def halo_split(i, _):
        splits(5 * i, halo[i])
        return 0

    lax.fori_loop(0, 2, halo_split, 0)
    e_low, e_high = edge_copy(1, 0, 1), edge_copy(2, 5, 1)
    e_low.start()
    e_high.start()

    for odd in range(2):
        for place in range(2):
            a = (3, 1, 2, 0)[2 * odd + place]
            block = wts[:, a * taps : (a + 1) * taps].astype(F32)
            wt_t[odd, :, place * n_out : (place + 1) * n_out] = block.T.astype(BF16)

    k_reduce(0)
    e_low.wait()
    e_high.wait()

    def build_halo(i, _):
        build(5 * i)
        return 0

    lax.fori_loop(0, 2, build_halo, 0)

    def forward(step, _):
        d, at = step // (area // 256), step % (area // 256)
        lanes = pl.ds(pl.multiple_of(at * 256, 256), 256)
        block = cols[pl.ds(2 * d, 4), :, :, :, lanes].reshape(4 * taps, 256)
        part = jnp.dot(wts[...], block, preferred_element_type=F32)
        fsum[d, :, lanes] = part
        fsend[d, :, lanes] = part.astype(BF16)
        return 0

    lax.fori_loop(0, 2 * (area // 256), forward, 0)

    def out_rows(ref, owner):
        return ref.at[:, pl.ds(pl.multiple_of(owner * local_out, local_out), local_out), :]

    f_copies = []
    for k in range(1, nx):
        peer = lax.rem(x + k, nx)
        f_copies.append(remote(out_rows(fsend, peer), frecv.at[k - 1], f_send.at[k - 1], f_recv.at[k - 1], {"ch": peer}))
        f_copies[-1].start()

    def outer_parts(index, _):
        kernel_part(1, index, 3 * index)
        return 0

    lax.fori_loop(0, 2, outer_parts, 0)
    k_pair(1).start()

    @pl.when(has_low)
    def _():
        g_down.wait_send()
        g_up.wait_recv()

    @pl.when(has_high)
    def _():
        g_up.wait_send()
        g_down.wait_recv()

    g_edge = remote(
        gbuf.at[:, :, pl.ds(pl.multiple_of(jnp.where(s == 0, area, 128), 128), 128)],
        gbuf.at[:, :, pl.ds(pl.multiple_of(jnp.where(s == 0, 0, 128 + area), 128), 128)],
        ge_sem.at[0], ge_sem.at[1], {"sub": other},
    )
    g_edge.start()

    g_edge.wait_send()
    remote(
        gbuf.at[:, :, pl.ds(0, 128)],
        gbuf.at[:, :, pl.ds(pl.multiple_of(jnp.where(s == 0, 128 + area, 0), 128), 128)],
        ge_sem.at[0], ge_sem.at[1], {"sub": other},
    ).wait_recv()

    lane = lax.broadcasted_iota(jnp.int32, (cin, 128), 1) % 64
    inner_low, inner_high = lane > 0, lane < 63
    weave = (l_at == 2 * (k_at % 64) + k_at // 64).astype(BF16)

    def volume_plane(step, _):
        pl.when(step == 1)(lambda: k_reduce(1))
        i = jnp.where(step < 2, step + 1, 3 * (step - 2))
        block = gbuf[pl.ds((i + 1) // 2, 2)].reshape(2 * n_out, 256 + area)
        wide[...] = jnp.dot(wt_t[i % 2], block, preferred_element_type=F32)

        def term(b, r, t):
            lanes = slice(t * 128, t * 128 + 128)

            def tap(e):
                return wide[(4 * b + e) * cin : (4 * b + e + 1) * cin, lanes]

            if r == 0:
                return tap(1) + jnp.where(inner_low, pltpu.roll(tap(3), 1, 1), 0.0)
            return tap(2) + jnp.where(inner_high, pltpu.roll(tap(0), 127, 1), 0.0)

        for q in range(2):
            kept = [None, None]
            for t in range(1, tiles + 1):
                both = []
                for r in range(2):
                    if q == 0:
                        before = pltpu.roll(term(3, r, t - 1), 64, 1) if kept[r] is None else kept[r]
                        after = pltpu.roll(term(3, r, t), 64, 1)
                        base = term(1, r, t)
                    else:
                        before = pltpu.roll(term(0, r, t), 64, 1) if kept[r] is None else kept[r]
                        after = pltpu.roll(term(0, r, t + 1), 64, 1)
                        base = term(2, r, t)
                    kept[r] = after
                    both.append(base + jnp.where(first, before, after))
                n = 2 * (t - 1)
                rows32[pl.ds(2 * n + q, cin, stride=pitch), :] = jnp.where(first, both[0], pltpu.roll(both[1], 64, 1))
                rows32[pl.ds(2 * n + 2 + q, cin, stride=pitch), :] = jnp.where(first, pltpu.roll(both[0], 64, 1), both[1])
        ready = rows32[...].reshape(cin, pitch, 128)[:, :high].reshape(cin * high, 128)
        woven = jnp.dot(ready.astype(BF16), weave, preferred_element_type=F32)
        vgrad[:, i] = woven.astype(BF16).reshape(cin, high, 128)
        return 0

    lax.fori_loop(0, 4, volume_plane, 0)

    for d in range(2):
        total = fsum[d, pl.ds(pl.multiple_of(x * local_out, local_out), local_out), :]
        for k in range(1, nx):
            if d == 0:
                f_copies[k - 1].wait()
            total = total + frecv[k - 1, d].astype(F32)
        feat[d] = total.astype(BF16)

    for group in range(2):
        result = krecv[group, z]
        for k in range(1, nz):
            k_copy(group, k).wait()
            result = result + kzin[group, k - 1, 0:rows, :].astype(F32)
        for index in range(2):
            a = (1 + index, 3 * index)[group]
            kgrad[:, a * taps : (a + 1) * taps] = result[:, index * taps : (index + 1) * taps]


def body(volume, kernel, cotangent):
    n_out, cin = kernel.shape[:2]
    nz, nx = lax.axis_size("sp"), lax.axis_size("ch")
    local_out, depth, area = cotangent.shape
    high = volume.shape[2]
    rows = n_out // (2 * nz)
    padded_rows = -(-rows // 16) * 16
    weights = kernel.transpose(0, 2, 1).reshape(n_out, 64 * cin)
    grads = cotangent.transpose(1, 0, 2)
    vmem = pl.BlockSpec(memory_space=pltpu.VMEM)
    dma = pltpu.SemaphoreType.DMA
    feat, vgrad, kgrad = pl.pallas_call(
        functools.partial(kernel_body, nz, nx),
        out_shape=(
            jax.ShapeDtypeStruct((depth, local_out, area), BF16),
            jax.ShapeDtypeStruct(volume.shape, BF16),
            jax.ShapeDtypeStruct((rows, 64 * cin), F32),
        ),
        in_specs=[vmem] * 3,
        out_specs=[vmem] * 3,
        scratch_shapes=[
            pltpu.VMEM((2, cin, high, 128), BF16),
            pltpu.VMEM((6, 2, cin * (high + 8), 128), F32),
            pltpu.VMEM((6, 2, cin, 128), BF16),
            pltpu.VMEM((6, 2, cin, 128), BF16),
            pltpu.VMEM((6, 4, 4, cin, area), BF16),
            pltpu.VMEM((4, n_out, 256 + area), BF16),
            pltpu.VMEM((depth, n_out, area), F32),
            pltpu.VMEM((depth, n_out, area), BF16),
            pltpu.VMEM((nx - 1, depth, local_out, area), BF16),
            pltpu.VMEM((2, nz, 2, rows, 32 * cin), F32),
            pltpu.VMEM((2, nz, rows, 32 * cin), F32),
            pltpu.VMEM((2, nz, padded_rows, 32 * cin), BF16),
            pltpu.VMEM((2, nz - 1, padded_rows, 32 * cin), BF16),
            pltpu.VMEM((16 * cin, 256 + area), F32),
            pltpu.VMEM((cin * (high + 8), 128), F32),
            pltpu.VMEM((2, 16 * cin, 2 * n_out), BF16),
            dma((2,)), dma((2,)),
            dma((nx - 1,)), dma((nx - 1,)),
            dma((2,)), dma((2,)),
            dma((3,)), dma((3,)),
            dma((2,)),
            dma((nx - 1,)), dma((nx - 1,)),
            dma((2, 2)),
            dma((2, nz - 1)), dma((2, nz - 1)),
            dma,
        ],
        compiler_params=pltpu.CompilerParams(
            collective_id=0, has_side_effects=True, vmem_limit_bytes=56 * 1024 * 1024
        ),
    )(volume, weights, grads)
    features = feat.transpose(1, 0, 2)
    kernel_grad = kgrad.reshape(rows, 64, cin).transpose(0, 2, 1)
    return (features, vgrad, kernel_grad)


def solution(mesh):
    return jax.shard_map(
        body,
        mesh=mesh,
        in_specs=(
            P("ch", ("grp", "sp"), "sub", None),
            P(None, "ch", None),
            P("ch", ("grp", "sp"), "sub"),
        ),
        out_specs=(
            P("ch", ("grp", "sp"), "sub"),
            P("ch", ("grp", "sp"), "sub", None),
            P(("grp", "sp", "sub"), "ch", None),
        ),
        check_vma=False,
    )
```

```python
import functools

import jax
import jax.numpy as jnp
from jax import lax
from jax.experimental import pallas as pl
from jax.experimental.pallas import tpu as pltpu
from jax.sharding import PartitionSpec as P

MESH = pl.DeviceIdType.MESH
F32 = jnp.float32
BF16 = jnp.bfloat16


def kernel_body(
    nz, nx, vol, wts, cot, feat, vgrad, kgrad,
    halo, split, edge_out, edge_in, cols, gbuf, fsum, fsend, frecv, kpart, krecv, ksend, kzin, wide, rows32, wt_t, wt, wrows,
    v_send, v_recv, g_send, g_recv, gz_send, gz_recv, e_send, e_recv, ge_sem, f_send, f_recv, ks_sem, kz_send, kz_recv, own_sem,
):
    z = lax.axis_index("sp")
    x = lax.axis_index("ch")
    s = lax.axis_index("sub")
    other = 1 - s
    cin = vol.shape[0]
    high = vol.shape[2]
    n_out = wts.shape[2]
    local_out = cot.shape[1]
    area = cot.shape[2]
    tiles = area // 128
    taps = 16 * cin
    pitch = high + 8
    has_low = z > 0
    has_high = z < nz - 1

    for side in (0, 128 + area):
        gbuf[:, :, side : side + 128] = jnp.zeros((4, n_out, 128), BF16)

    @pl.when(jnp.logical_not(has_low))
    def _():
        halo[0] = jnp.zeros(halo.shape[1:], BF16)
        gbuf[0] = jnp.zeros(gbuf.shape[1:], BF16)

    @pl.when(jnp.logical_not(has_high))
    def _():
        halo[1] = jnp.zeros(halo.shape[1:], BF16)
        gbuf[3] = jnp.zeros(gbuf.shape[1:], BF16)

    barrier = pltpu.get_barrier_semaphore()
    for k in range(1, nz):
        pl.semaphore_signal(barrier, 1, device_id={"sp": lax.rem(z + k, nz)}, device_id_type=MESH)
    for k in range(1, nx):
        pl.semaphore_signal(barrier, 1, device_id={"ch": lax.rem(x + k, nx)}, device_id_type=MESH)
    pl.semaphore_signal(barrier, 1, device_id={"sub": other}, device_id_type=MESH)

    k_at = lax.broadcasted_iota(jnp.int32, (128, 128), 0)
    l_at = lax.broadcasted_iota(jnp.int32, (128, 128), 1)
    pick = [
        (k_at == 2 * (l_at % 64) + (l_at // 64 + 2 * half) - 1).astype(BF16) for half in range(2)
    ]
    first = lax.broadcasted_iota(jnp.int32, (cin, 128), 1) < 64

    def splits(plane, cells):
        flat = cells.reshape(cin * high, 128)
        for half in range(2):
            value = jnp.dot(flat, pick[half], preferred_element_type=F32)
            for c in range(cin):
                split[plane, half, c * pitch : c * pitch + high, :] = value[c * high : (c + 1) * high]
            rim = jnp.where(
                s == 0,
                split.at[plane, half][pl.ds(high - 1, cin, stride=pitch), :],
                split.at[plane, half][pl.ds(0, cin, stride=pitch), :],
            )
            edge_out[plane, half] = rim.astype(BF16)

    def own_split(i, _):
        splits(i + 1, vol[:, i])
        return 0

    lax.fori_loop(0, 4, own_split, 0)

    pl.semaphore_wait(barrier, nz + nx - 1)

    def remote(src, dst, send, recv, target):
        return pltpu.make_async_remote_copy(
            src_ref=src, dst_ref=dst, send_sem=send, recv_sem=recv, device_id=target, device_id_type=MESH
        )

    low = jnp.maximum(z - 1, 0)
    up = jnp.minimum(z + 1, nz - 1)
    v_down = remote(vol.at[:, 0], halo.at[1], v_send.at[0], v_recv.at[1], {"sp": low})
    v_up = remote(vol.at[:, 3], halo.at[0], v_send.at[1], v_recv.at[0], {"sp": up})
    pl.when(has_low)(v_down.start)
    pl.when(has_high)(v_up.start)

    def g_rows(owner):
        return gbuf.at[pl.ds(1, 2), pl.ds(pl.multiple_of(owner * local_out, local_out), local_out), pl.ds(128, area)]

    g_copies = []
    for k in range(1, nx):
        g_copies.append(remote(cot, g_rows(x), g_send.at[k - 1], g_recv.at[k - 1], {"ch": lax.rem(x + k, nx)}))
        g_copies[-1].start()
    own = pltpu.make_async_copy(cot, g_rows(x), own_sem)
    own.start()

    def edge_copy(index, start, count):
        return remote(
            edge_out.at[pl.ds(start, count)], edge_in.at[pl.ds(start, count)],
            e_send.at[index], e_recv.at[index], {"sub": other},
        )

    e_own = edge_copy(0, 1, 4)
    e_own.start()

    step = 64 + 8
    for c in range(cin):
        wrows[c * step : c * step + 64, :] = wts[c].astype(F32)
    for tap in range(64):
        odd, place = ((1, 1), (0, 1), (1, 0), (0, 0))[tap // 16]
        block = wrows[pl.ds(tap, cin, stride=step), :]
        wt_t[odd, (tap % 16) * cin : (tap % 16 + 1) * cin, place * n_out : (place + 1) * n_out] = block.astype(BF16)
    for a in range(4):
        odd, place = ((1, 1), (0, 1), (1, 0), (0, 0))[a]
        block = wt_t[odd, :, place * n_out : (place + 1) * n_out].astype(F32)
        wt[:, a * taps : (a + 1) * taps] = block.T.astype(BF16)

    def build(plane):
        for half in range(2):
            rim = edge_in[plane, half].astype(F32)
            above = jnp.where(s == 1, rim, 0.0)
            below = jnp.where(s == 0, rim, 0.0)

            def row(j):
                if j < 0:
                    return above
                if j >= high:
                    return below
                return split.at[plane, half][pl.ds(j, cin, stride=pitch), :]

            for start in (-1, 0):
                a_row = row(start)
                a_turned = pltpu.roll(a_row, 64, 1)
                for j in range(start, high - 1, 2):
                    b_row = row(j + 2)
                    b_turned = pltpu.roll(b_row, 64, 1)
                    b, t = (j + 1) % 4, (j + 1) // 4
                    lanes = slice(t * 128, t * 128 + 128)
                    cols[plane, b, 2 * half, :, lanes] = jnp.where(first, a_row, b_turned).astype(BF16)
                    cols[plane, b, 2 * half + 1, :, lanes] = jnp.where(first, a_turned, b_row).astype(BF16)
                    a_row, a_turned = b_row, b_turned

    def g_plane(at):
        return gbuf.at[at, :, pl.ds(128, area)]

    g_down = remote(g_plane(1), g_plane(3), gz_send.at[0], gz_recv.at[1], {"sp": low})
    g_up = remote(g_plane(2), g_plane(0), gz_send.at[1], gz_recv.at[0], {"sp": up})
    def rim_lanes(at):
        return pl.ds(pl.multiple_of(at, 128), 128)

    def g_edge(index, start, count):
        planes = pl.ds(start, count)
        return remote(
            gbuf.at[planes, :, rim_lanes(jnp.where(s == 0, area, 128))],
            gbuf.at[planes, :, rim_lanes(jnp.where(s == 0, 0, 128 + area))],
            ge_sem.at[0, index], ge_sem.at[1, index], {"sub": other},
        )

    def g_edge_wait(index, start, count):
        planes = pl.ds(start, count)
        g_edge(index, start, count).wait_send()
        remote(
            gbuf.at[planes, :, rim_lanes(jnp.where(s == 0, area, 128))],
            gbuf.at[planes, :, rim_lanes(jnp.where(s == 0, 128 + area, 0))],
            ge_sem.at[0, index], ge_sem.at[1, index], {"sub": other},
        ).wait_recv()

    def outer_planes():
        @pl.when(has_low)
        def _():
            g_down.wait_send()
            g_up.wait_recv()

        @pl.when(has_high)
        def _():
            g_up.wait_send()
            g_down.wait_recv()
        g_edge(1, 0, 1).start()
        g_edge(2, 3, 1).start()

    def outer_rims():
        g_edge_wait(1, 0, 1)
        g_edge_wait(2, 3, 1)

    def spread():
        own.wait()
        for k in range(1, nx):
            g_copies[k - 1].wait_send()
            origin = lax.rem(x + nx - k, nx)
            remote(cot, g_rows(origin), g_send.at[k - 1], g_recv.at[k - 1], {"ch": origin}).wait_recv()
        pl.when(has_low)(g_down.start)
        pl.when(has_high)(g_up.start)
        g_edge(0, 1, 2).start()

    def build_own(i, _):
        pl.when(i == 3)(spread)
        build(i + 1)
        return 0

    e_own.wait()
    lax.fori_loop(0, 4, build_own, 0)

    rows = n_out // (2 * nz)

    def kernel_part(group, index, a):
        total = 0.0
        for d in range(2):
            total += lax.dot_general(
                gbuf[1 + d, :, 128 : 128 + area],
                cols[2 * d + a].reshape(taps, area),
                (((1,), (1,)), ((), ())),
                preferred_element_type=F32,
            )
        lanes = pl.ds(pl.multiple_of(index * taps, 128), taps)
        for block in range(2 * nz):
            kpart[group, block // 2, block % 2, :, lanes] = total[block * rows : (block + 1) * rows]

    def k_pair(group):
        return remote(
            kpart.at[group, :, other], krecv.at[group], ks_sem.at[0, group], ks_sem.at[1, group], {"sub": other}
        )

    def k_copy(group, k):
        peer = lax.rem(z + k, nz)
        return remote(
            ksend.at[group, peer], kzin.at[group, k - 1],
            kz_send.at[group, k - 1], kz_recv.at[group, k - 1], {"sp": peer},
        )

    def k_reduce(group):
        k_pair(group).wait()
        for block in range(nz):
            mine = jnp.where(s == 0, kpart[group, block, 0], kpart[group, block, 1]) + krecv[group, block]
            krecv[group, block] = mine
            ksend[group, block, 0:rows, :] = mine.astype(BF16)
        for k in range(1, nz):
            k_copy(group, k).start()

    def inner_parts(index, _):
        kernel_part(0, index, 1 + index)
        return 0

    lax.fori_loop(0, 2, inner_parts, 0)
    k_pair(0).start()

    @pl.when(has_low)
    def _():
        v_down.wait_send()
        v_up.wait_recv()

    @pl.when(has_high)
    def _():
        v_up.wait_send()
        v_down.wait_recv()

    def halo_split(i, _):
        splits(5 * i, halo[i])
        return 0

    lax.fori_loop(0, 2, halo_split, 0)
    e_low, e_high = edge_copy(1, 0, 1), edge_copy(2, 5, 1)
    e_low.start()
    e_high.start()

    k_reduce(0)
    e_low.wait()
    e_high.wait()

    def build_halo(i, _):
        build(5 * i)
        return 0

    lax.fori_loop(0, 2, build_halo, 0)


    def forward(step, _):
        d, at = step // (area // 256), step % (area // 256)
        lanes = pl.ds(pl.multiple_of(at * 256, 256), 256)
        block = cols[pl.ds(2 * d, 4), :, :, :, lanes].reshape(4 * taps, 256)
        part = jnp.dot(wt[...], block, preferred_element_type=F32)
        fsum[d, :, lanes] = part
        fsend[d, :, lanes] = part.astype(BF16)
        return 0

    lax.fori_loop(0, 2 * (area // 256), forward, 0)

    def out_rows(ref, owner):
        return ref.at[:, pl.ds(pl.multiple_of(owner * local_out, local_out), local_out), :]

    f_copies = []
    for k in range(1, nx):
        peer = lax.rem(x + k, nx)
        f_copies.append(remote(out_rows(fsend, peer), frecv.at[k - 1], f_send.at[k - 1], f_recv.at[k - 1], {"ch": peer}))
        f_copies[-1].start()

    def outer_parts(index, _):
        kernel_part(1, index, 3 * index)
        return 0

    lax.fori_loop(0, 2, outer_parts, 0)
    k_pair(1).start()


    g_edge_wait(0, 1, 2)

    lane = lax.broadcasted_iota(jnp.int32, (cin, 128), 1) % 64
    inner_low, inner_high = lane > 0, lane < 63
    weave = (l_at == 2 * (k_at % 64) + k_at // 64).astype(BF16)

    def volume_plane(step, _):
        pl.when(step == 1)(lambda: k_reduce(1))
        pl.when(step == 1)(outer_planes)
        pl.when(step == 2)(outer_rims)
        i = jnp.where(step < 2, step + 1, 3 * (step - 2))
        block = gbuf[pl.ds((i + 1) // 2, 2)].reshape(2 * n_out, 256 + area)
        wide[...] = jnp.dot(wt_t[i % 2], block, preferred_element_type=F32)

        def term(b, r, t):
            lanes = slice(t * 128, t * 128 + 128)

            def tap(e):
                return wide[(4 * b + e) * cin : (4 * b + e + 1) * cin, lanes]

            if r == 0:
                return tap(1) + jnp.where(inner_low, pltpu.roll(tap(3), 1, 1), 0.0)
            return tap(2) + jnp.where(inner_high, pltpu.roll(tap(0), 127, 1), 0.0)

        for q in range(2):
            kept = [None, None]
            for t in range(1, tiles + 1):
                both = []
                for r in range(2):
                    if q == 0:
                        before = pltpu.roll(term(3, r, t - 1), 64, 1) if kept[r] is None else kept[r]
                        after = pltpu.roll(term(3, r, t), 64, 1)
                        base = term(1, r, t)
                    else:
                        before = pltpu.roll(term(0, r, t), 64, 1) if kept[r] is None else kept[r]
                        after = pltpu.roll(term(0, r, t + 1), 64, 1)
                        base = term(2, r, t)
                    kept[r] = after
                    both.append(base + jnp.where(first, before, after))
                n = 2 * (t - 1)
                rows32[pl.ds(2 * n + q, cin, stride=pitch), :] = jnp.where(first, both[0], pltpu.roll(both[1], 64, 1))
                rows32[pl.ds(2 * n + 2 + q, cin, stride=pitch), :] = jnp.where(first, pltpu.roll(both[0], 64, 1), both[1])
        ready = rows32[...].reshape(cin, pitch, 128)[:, :high].reshape(cin * high, 128)
        woven = jnp.dot(ready.astype(BF16), weave, preferred_element_type=F32)
        vgrad[:, i] = woven.astype(BF16).reshape(cin, high, 128)
        return 0

    lax.fori_loop(0, 4, volume_plane, 0)

    for d in range(2):
        total = fsum[d, pl.ds(pl.multiple_of(x * local_out, local_out), local_out), :]
        for k in range(1, nx):
            if d == 0:
                f_copies[k - 1].wait()
            total = total + frecv[k - 1, d].astype(F32)
        feat[d] = total.astype(BF16)

    for group in range(2):
        result = krecv[group, z]
        for k in range(1, nz):
            k_copy(group, k).wait()
            result = result + kzin[group, k - 1, 0:rows, :].astype(F32)
        for index in range(2):
            a = (1 + index, 3 * index)[group]
            kgrad[:, a * taps : (a + 1) * taps] = result[:, index * taps : (index + 1) * taps]


def body(volume, kernel, cotangent):
    n_out, cin = kernel.shape[:2]
    nz, nx = lax.axis_size("sp"), lax.axis_size("ch")
    local_out, depth, area = cotangent.shape
    high = volume.shape[2]
    rows = n_out // (2 * nz)
    padded_rows = -(-rows // 16) * 16
    weights = kernel.transpose(1, 2, 0)
    grads = cotangent.transpose(1, 0, 2)
    vmem = pl.BlockSpec(memory_space=pltpu.VMEM)
    dma = pltpu.SemaphoreType.DMA
    feat, vgrad, kgrad = pl.pallas_call(
        functools.partial(kernel_body, nz, nx),
        out_shape=(
            jax.ShapeDtypeStruct((depth, local_out, area), BF16),
            jax.ShapeDtypeStruct(volume.shape, BF16),
            jax.ShapeDtypeStruct((rows, 64 * cin), F32),
        ),
        in_specs=[vmem] * 3,
        out_specs=[vmem] * 3,
        scratch_shapes=[
            pltpu.VMEM((2, cin, high, 128), BF16),
            pltpu.VMEM((6, 2, cin * (high + 8), 128), F32),
            pltpu.VMEM((6, 2, cin, 128), BF16),
            pltpu.VMEM((6, 2, cin, 128), BF16),
            pltpu.VMEM((6, 4, 4, cin, area), BF16),
            pltpu.VMEM((4, n_out, 256 + area), BF16),
            pltpu.VMEM((depth, n_out, area), F32),
            pltpu.VMEM((depth, n_out, area), BF16),
            pltpu.VMEM((nx - 1, depth, local_out, area), BF16),
            pltpu.VMEM((2, nz, 2, rows, 32 * cin), F32),
            pltpu.VMEM((2, nz, rows, 32 * cin), F32),
            pltpu.VMEM((2, nz, padded_rows, 32 * cin), BF16),
            pltpu.VMEM((2, nz - 1, padded_rows, 32 * cin), BF16),
            pltpu.VMEM((16 * cin, 256 + area), F32),
            pltpu.VMEM((cin * (high + 8), 128), F32),
            pltpu.VMEM((2, 16 * cin, 2 * n_out), BF16),
            pltpu.VMEM((n_out, 64 * cin), BF16),
            pltpu.VMEM((cin * (64 + 8), n_out), F32),
            dma((2,)), dma((2,)),
            dma((nx - 1,)), dma((nx - 1,)),
            dma((2,)), dma((2,)),
            dma((3,)), dma((3,)),
            dma((2, 3)),
            dma((nx - 1,)), dma((nx - 1,)),
            dma((2, 2)),
            dma((2, nz - 1)), dma((2, nz - 1)),
            dma,
        ],
        compiler_params=pltpu.CompilerParams(
            collective_id=0, has_side_effects=True, vmem_limit_bytes=56 * 1024 * 1024
        ),
    )(volume, weights, grads)
    features = feat.transpose(1, 0, 2)
    kernel_grad = kgrad.reshape(rows, 64, cin).transpose(0, 2, 1)
    return (features, vgrad, kernel_grad)


def solution(mesh):
    return jax.shard_map(
        body,
        mesh=mesh,
        in_specs=(
            P("ch", ("grp", "sp"), "sub", None),
            P(None, "ch", None),
            P("ch", ("grp", "sp"), "sub"),
        ),
        out_specs=(
            P("ch", ("grp", "sp"), "sub"),
            P("ch", ("grp", "sp"), "sub", None),
            P(("grp", "sp", "sub"), "ch", None),
        ),
        check_vma=False,
    )
```

```python
import functools

import jax
import jax.numpy as jnp
from jax import lax
from jax.experimental import pallas as pl
from jax.experimental.pallas import tpu as pltpu
from jax.sharding import PartitionSpec as P

MESH = pl.DeviceIdType.MESH
F32 = jnp.float32
BF16 = jnp.bfloat16


def kernel_body(
    nz, nx, vol, wts, cot, feat, vgrad, kgrad,
    halo, split, edge_out, edge_in, cols, gbuf, fsum, fsend, frecv, kpart, krecv, ksend, kzin, wide, rows32, wt_t, wt, wrows,
    v_send, v_recv, g_send, g_recv, gz_send, gz_recv, e_send, e_recv, ge_sem, f_send, f_recv, ks_sem, kz_send, kz_recv, own_sem,
):
    z = lax.axis_index("sp")
    x = lax.axis_index("ch")
    s = lax.axis_index("sub")
    other = 1 - s
    cin = vol.shape[0]
    high = vol.shape[2]
    n_out = wts.shape[2]
    local_out = cot.shape[1]
    area = cot.shape[2]
    tiles = area // 128
    taps = 16 * cin
    pitch = high + 8
    has_low = z > 0
    has_high = z < nz - 1

    for side in (0, 128 + area):
        gbuf[:, :, side : side + 128] = jnp.zeros((4, n_out, 128), BF16)

    @pl.when(jnp.logical_not(has_low))
    def _():
        halo[0] = jnp.zeros(halo.shape[1:], BF16)
        gbuf[0] = jnp.zeros(gbuf.shape[1:], BF16)

    @pl.when(jnp.logical_not(has_high))
    def _():
        halo[1] = jnp.zeros(halo.shape[1:], BF16)
        gbuf[3] = jnp.zeros(gbuf.shape[1:], BF16)

    barrier = pltpu.get_barrier_semaphore()
    for k in range(1, nz):
        pl.semaphore_signal(barrier, 1, device_id={"sp": lax.rem(z + k, nz)}, device_id_type=MESH)
    for k in range(1, nx):
        pl.semaphore_signal(barrier, 1, device_id={"ch": lax.rem(x + k, nx)}, device_id_type=MESH)
    pl.semaphore_signal(barrier, 1, device_id={"sub": other}, device_id_type=MESH)

    k_at = lax.broadcasted_iota(jnp.int32, (128, 128), 0)
    l_at = lax.broadcasted_iota(jnp.int32, (128, 128), 1)
    pick = [
        (k_at == 2 * (l_at % 64) + (l_at // 64 + 2 * half) - 1).astype(BF16) for half in range(2)
    ]
    first = lax.broadcasted_iota(jnp.int32, (cin, 128), 1) < 64

    def splits(plane, cells):
        flat = cells.reshape(cin * high, 128)
        for half in range(2):
            value = jnp.dot(flat, pick[half], preferred_element_type=F32)
            for c in range(cin):
                split[plane, half, c * pitch : c * pitch + high, :] = value[c * high : (c + 1) * high]
            rim = jnp.where(
                s == 0,
                split.at[plane, half][pl.ds(high - 1, cin, stride=pitch), :],
                split.at[plane, half][pl.ds(0, cin, stride=pitch), :],
            )
            edge_out[plane, half] = rim.astype(BF16)

    def own_split(i, _):
        splits(i + 1, vol[:, i])
        return 0

    lax.fori_loop(0, 4, own_split, 0)

    pl.semaphore_wait(barrier, nz + nx - 1)

    def remote(src, dst, send, recv, target):
        return pltpu.make_async_remote_copy(
            src_ref=src, dst_ref=dst, send_sem=send, recv_sem=recv, device_id=target, device_id_type=MESH
        )

    low = jnp.maximum(z - 1, 0)
    up = jnp.minimum(z + 1, nz - 1)
    v_down = remote(vol.at[:, 0], halo.at[1], v_send.at[0], v_recv.at[1], {"sp": low})
    v_up = remote(vol.at[:, 3], halo.at[0], v_send.at[1], v_recv.at[0], {"sp": up})
    pl.when(has_low)(v_down.start)
    pl.when(has_high)(v_up.start)

    def g_rows(owner):
        return gbuf.at[pl.ds(1, 2), pl.ds(pl.multiple_of(owner * local_out, local_out), local_out), pl.ds(128, area)]

    g_copies = []
    for k in range(1, nx):
        g_copies.append(remote(cot, g_rows(x), g_send.at[k - 1], g_recv.at[k - 1], {"ch": lax.rem(x + k, nx)}))
        g_copies[-1].start()
    own = pltpu.make_async_copy(cot, g_rows(x), own_sem)
    own.start()

    def edge_copy(index, start, count):
        return remote(
            edge_out.at[pl.ds(start, count)], edge_in.at[pl.ds(start, count)],
            e_send.at[index], e_recv.at[index], {"sub": other},
        )

    e_own = edge_copy(0, 1, 4)
    e_own.start()

    step = 64 + 8
    for c in range(cin):
        wrows[c * step : c * step + 64, :] = wts[c].astype(F32)
    for tap in range(64):
        odd, place = ((1, 1), (0, 1), (1, 0), (0, 0))[tap // 16]
        block = wrows[pl.ds(tap, cin, stride=step), :]
        wt_t[odd, (tap % 16) * cin : (tap % 16 + 1) * cin, place * n_out : (place + 1) * n_out] = block.astype(BF16)
    for a in range(4):
        odd, place = ((1, 1), (0, 1), (1, 0), (0, 0))[a]
        block = wt_t[odd, :, place * n_out : (place + 1) * n_out].astype(F32)
        wt[:, a * taps : (a + 1) * taps] = block.T.astype(BF16)

    def build(plane):
        for half in range(2):
            rim = edge_in[plane, half].astype(F32)
            above = jnp.where(s == 1, rim, 0.0)
            below = jnp.where(s == 0, rim, 0.0)

            def row(j):
                if j < 0:
                    return above
                if j >= high:
                    return below
                return split.at[plane, half][pl.ds(j, cin, stride=pitch), :]

            for start in (-1, 0):
                a_row = row(start)
                a_turned = pltpu.roll(a_row, 64, 1)
                for j in range(start, high - 1, 2):
                    b_row = row(j + 2)
                    b_turned = pltpu.roll(b_row, 64, 1)
                    b, t = (j + 1) % 4, (j + 1) // 4
                    lanes = slice(t * 128, t * 128 + 128)
                    cols[plane, b, 2 * half, :, lanes] = jnp.where(first, a_row, b_turned).astype(BF16)
                    cols[plane, b, 2 * half + 1, :, lanes] = jnp.where(first, a_turned, b_row).astype(BF16)
                    a_row, a_turned = b_row, b_turned

    def g_plane(at):
        return gbuf.at[at, :, pl.ds(128, area)]

    g_down = remote(g_plane(1), g_plane(3), gz_send.at[0], gz_recv.at[1], {"sp": low})
    g_up = remote(g_plane(2), g_plane(0), gz_send.at[1], gz_recv.at[0], {"sp": up})
    def rim_lanes(at):
        return pl.ds(pl.multiple_of(at, 128), 128)

    def g_edge(index, start, count):
        planes = pl.ds(start, count)
        return remote(
            gbuf.at[planes, :, rim_lanes(jnp.where(s == 0, area, 128))],
            gbuf.at[planes, :, rim_lanes(jnp.where(s == 0, 0, 128 + area))],
            ge_sem.at[0, index], ge_sem.at[1, index], {"sub": other},
        )

    def g_edge_wait(index, start, count):
        planes = pl.ds(start, count)
        g_edge(index, start, count).wait_send()
        remote(
            gbuf.at[planes, :, rim_lanes(jnp.where(s == 0, area, 128))],
            gbuf.at[planes, :, rim_lanes(jnp.where(s == 0, 128 + area, 0))],
            ge_sem.at[0, index], ge_sem.at[1, index], {"sub": other},
        ).wait_recv()

    def outer_planes():
        @pl.when(has_low)
        def _():
            g_down.wait_send()
            g_up.wait_recv()

        @pl.when(has_high)
        def _():
            g_up.wait_send()
            g_down.wait_recv()
        g_edge(1, 0, 1).start()
        g_edge(2, 3, 1).start()

    def outer_rims():
        g_edge_wait(1, 0, 1)
        g_edge_wait(2, 3, 1)

    def spread():
        own.wait()
        for k in range(1, nx):
            g_copies[k - 1].wait_send()
            origin = lax.rem(x + nx - k, nx)
            remote(cot, g_rows(origin), g_send.at[k - 1], g_recv.at[k - 1], {"ch": origin}).wait_recv()
        pl.when(has_low)(g_down.start)
        pl.when(has_high)(g_up.start)
        g_edge(0, 1, 2).start()

    def build_own(i, _):
        pl.when(i == 3)(spread)
        build(i + 1)
        return 0

    e_own.wait()
    lax.fori_loop(0, 4, build_own, 0)

    rows = n_out // (2 * nz)

    def kernel_part(group, index, a):
        total = 0.0
        for d in range(2):
            total += lax.dot_general(
                gbuf[1 + d, :, 128 : 128 + area],
                cols[2 * d + a].reshape(taps, area),
                (((1,), (1,)), ((), ())),
                preferred_element_type=F32,
            )
        lanes = pl.ds(pl.multiple_of(index * taps, 128), taps)
        for block in range(2 * nz):
            kpart[group, block // 2, block % 2, :, lanes] = total[block * rows : (block + 1) * rows]

    def k_pair(group):
        return remote(
            kpart.at[group, :, other], krecv.at[group], ks_sem.at[0, group], ks_sem.at[1, group], {"sub": other}
        )

    def k_copy(group, k):
        peer = lax.rem(z + k, nz)
        return remote(
            ksend.at[group, peer], kzin.at[group, k - 1],
            kz_send.at[group, k - 1], kz_recv.at[group, k - 1], {"sp": peer},
        )

    def k_reduce(group):
        k_pair(group).wait()
        for block in range(nz):
            mine = jnp.where(s == 0, kpart[group, block, 0], kpart[group, block, 1]) + krecv[group, block]
            krecv[group, block] = mine
            ksend[group, block, 0:rows, :] = mine.astype(BF16)
        for k in range(1, nz):
            k_copy(group, k).start()

    def inner_parts(index, _):
        kernel_part(0, index, 1 + index)
        return 0

    lax.fori_loop(0, 2, inner_parts, 0)
    k_pair(0).start()

    @pl.when(has_low)
    def _():
        v_down.wait_send()
        v_up.wait_recv()

    @pl.when(has_high)
    def _():
        v_up.wait_send()
        v_down.wait_recv()

    def halo_split(i, _):
        splits(5 * i, halo[i])
        return 0

    lax.fori_loop(0, 2, halo_split, 0)
    e_low, e_high = edge_copy(1, 0, 1), edge_copy(2, 5, 1)
    e_low.start()
    e_high.start()

    k_reduce(0)
    e_low.wait()
    e_high.wait()

    def build_halo(i, _):
        build(5 * i)
        return 0

    lax.fori_loop(0, 2, build_halo, 0)


    def forward(step, _):
        d, at = step // (area // 256), step % (area // 256)
        lanes = pl.ds(pl.multiple_of(at * 256, 256), 256)
        block = cols[pl.ds(2 * d, 4), :, :, :, lanes].reshape(4 * taps, 256)
        part = jnp.dot(wt[...], block, preferred_element_type=F32)
        fsum[d, :, lanes] = part
        fsend[d, :, lanes] = part.astype(BF16)
        return 0

    lax.fori_loop(0, 2 * (area // 256), forward, 0)

    def out_rows(ref, owner):
        return ref.at[:, pl.ds(pl.multiple_of(owner * local_out, local_out), local_out), :]

    f_copies = []
    for k in range(1, nx):
        peer = lax.rem(x + k, nx)
        f_copies.append(remote(out_rows(fsend, peer), frecv.at[k - 1], f_send.at[k - 1], f_recv.at[k - 1], {"ch": peer}))
        f_copies[-1].start()

    def outer_parts(index, _):
        kernel_part(1, index, 3 * index)
        return 0

    lax.fori_loop(0, 2, outer_parts, 0)
    k_pair(1).start()


    g_edge_wait(0, 1, 2)

    lane = lax.broadcasted_iota(jnp.int32, (cin, 128), 1) % 64
    inner_low, inner_high = lane > 0, lane < 63
    weave = (l_at == 2 * (k_at % 64) + k_at // 64).astype(BF16)

    def volume_plane(step, _):
        pl.when(step == 1)(outer_planes)
        pl.when(step == 1)(lambda: k_reduce(1))
        pl.when(step == 2)(outer_rims)
        i = jnp.where(step < 2, step + 1, 3 * (step - 2))
        block = gbuf[pl.ds((i + 1) // 2, 2)].reshape(2 * n_out, 256 + area)
        wide[...] = jnp.dot(wt_t[i % 2], block, preferred_element_type=F32)

        def term(b, r, t):
            lanes = slice(t * 128, t * 128 + 128)

            def tap(e):
                return wide[(4 * b + e) * cin : (4 * b + e + 1) * cin, lanes]

            if r == 0:
                return tap(1) + jnp.where(inner_low, pltpu.roll(tap(3), 1, 1), 0.0)
            return tap(2) + jnp.where(inner_high, pltpu.roll(tap(0), 127, 1), 0.0)

        for q in range(2):
            kept = [None, None]
            for t in range(1, tiles + 1):
                both = []
                for r in range(2):
                    if q == 0:
                        before = pltpu.roll(term(3, r, t - 1), 64, 1) if kept[r] is None else kept[r]
                        after = pltpu.roll(term(3, r, t), 64, 1)
                        base = term(1, r, t)
                    else:
                        before = pltpu.roll(term(0, r, t), 64, 1) if kept[r] is None else kept[r]
                        after = pltpu.roll(term(0, r, t + 1), 64, 1)
                        base = term(2, r, t)
                    kept[r] = after
                    both.append(base + jnp.where(first, before, after))
                n = 2 * (t - 1)
                rows32[pl.ds(2 * n + q, cin, stride=pitch), :] = jnp.where(first, both[0], pltpu.roll(both[1], 64, 1))
                rows32[pl.ds(2 * n + 2 + q, cin, stride=pitch), :] = jnp.where(first, pltpu.roll(both[0], 64, 1), both[1])
        ready = rows32[...].reshape(cin, pitch, 128)[:, :high].reshape(cin * high, 128)
        woven = jnp.dot(ready.astype(BF16), weave, preferred_element_type=F32)
        vgrad[:, i] = woven.astype(BF16).reshape(cin, high, 128)
        return 0

    lax.fori_loop(0, 4, volume_plane, 0)

    for d in range(2):
        total = fsum[d, pl.ds(pl.multiple_of(x * local_out, local_out), local_out), :]
        for k in range(1, nx):
            if d == 0:
                f_copies[k - 1].wait()
            total = total + frecv[k - 1, d].astype(F32)
        feat[d] = total.astype(BF16)

    for group in range(2):
        result = krecv[group, z]
        for k in range(1, nz):
            k_copy(group, k).wait()
            result = result + kzin[group, k - 1, 0:rows, :].astype(F32)
        for index in range(2):
            a = (1 + index, 3 * index)[group]
            kgrad[:, a * taps : (a + 1) * taps] = result[:, index * taps : (index + 1) * taps]


def body(volume, kernel, cotangent):
    n_out, cin = kernel.shape[:2]
    nz, nx = lax.axis_size("sp"), lax.axis_size("ch")
    local_out, depth, area = cotangent.shape
    high = volume.shape[2]
    rows = n_out // (2 * nz)
    padded_rows = -(-rows // 16) * 16
    weights = kernel.transpose(1, 2, 0)
    grads = cotangent.transpose(1, 0, 2)
    vmem = pl.BlockSpec(memory_space=pltpu.VMEM)
    dma = pltpu.SemaphoreType.DMA
    feat, vgrad, kgrad = pl.pallas_call(
        functools.partial(kernel_body, nz, nx),
        out_shape=(
            jax.ShapeDtypeStruct((depth, local_out, area), BF16),
            jax.ShapeDtypeStruct(volume.shape, BF16),
            jax.ShapeDtypeStruct((rows, 64 * cin), F32),
        ),
        in_specs=[vmem] * 3,
        out_specs=[vmem] * 3,
        scratch_shapes=[
            pltpu.VMEM((2, cin, high, 128), BF16),
            pltpu.VMEM((6, 2, cin * (high + 8), 128), F32),
            pltpu.VMEM((6, 2, cin, 128), BF16),
            pltpu.VMEM((6, 2, cin, 128), BF16),
            pltpu.VMEM((6, 4, 4, cin, area), BF16),
            pltpu.VMEM((4, n_out, 256 + area), BF16),
            pltpu.VMEM((depth, n_out, area), F32),
            pltpu.VMEM((depth, n_out, area), BF16),
            pltpu.VMEM((nx - 1, depth, local_out, area), BF16),
            pltpu.VMEM((2, nz, 2, rows, 32 * cin), F32),
            pltpu.VMEM((2, nz, rows, 32 * cin), F32),
            pltpu.VMEM((2, nz, padded_rows, 32 * cin), BF16),
            pltpu.VMEM((2, nz - 1, padded_rows, 32 * cin), BF16),
            pltpu.VMEM((16 * cin, 256 + area), F32),
            pltpu.VMEM((cin * (high + 8), 128), F32),
            pltpu.VMEM((2, 16 * cin, 2 * n_out), BF16),
            pltpu.VMEM((n_out, 64 * cin), BF16),
            pltpu.VMEM((cin * (64 + 8), n_out), F32),
            dma((2,)), dma((2,)),
            dma((nx - 1,)), dma((nx - 1,)),
            dma((2,)), dma((2,)),
            dma((3,)), dma((3,)),
            dma((2, 3)),
            dma((nx - 1,)), dma((nx - 1,)),
            dma((2, 2)),
            dma((2, nz - 1)), dma((2, nz - 1)),
            dma,
        ],
        compiler_params=pltpu.CompilerParams(
            collective_id=0, has_side_effects=True, vmem_limit_bytes=56 * 1024 * 1024
        ),
    )(volume, weights, grads)
    features = feat.transpose(1, 0, 2)
    kernel_grad = kgrad.reshape(rows, 64, cin).transpose(0, 2, 1)
    return (features, vgrad, kernel_grad)


def solution(mesh):
    return jax.shard_map(
        body,
        mesh=mesh,
        in_specs=(
            P("ch", ("grp", "sp"), "sub", None),
            P(None, "ch", None),
            P("ch", ("grp", "sp"), "sub"),
        ),
        out_specs=(
            P("ch", ("grp", "sp"), "sub"),
            P("ch", ("grp", "sp"), "sub", None),
            P(("grp", "sp", "sub"), "ch", None),
        ),
        check_vma=False,
    )
```
